32 devices in a mesh: dp: 4 (over y, core), expert: 8 (over z, x).
Axes of the slice: x: 2, y: 2, z: 4, core: 2. Of those that a mesh axis runs over, the one named last changes fastest.
Arguments:
- hidden_token_tiles: bfloat16 [4, 512, 1024], P(None, 'dp'), may hold values from -6 to 6
- gradient_token_tiles: bfloat16 [4, 7168, 512], P(None, 'expert', 'dp'), may hold values from -0.59765625 to 0.59765625
- momentum: float32 [4, 7168, 1024], P('dp', 'expert'), may hold values from -54 to 54, as said below
- filled_tile_count: int32 [4, 4], replicated, may hold values from 1 to 8, as said below
Outputs:
- new_momentum: float32 [4, 7168, 1024], P('dp', 'expert')
- update: float32 [4, 7168, 1024], P(None, 'expert')
The draws below stay inside these ranges and needn't reach their ends.
Inputs may be any that keep to these rules, and one draw needn't show every extreme that they name: momentum entries are finite reals. filled_tile_count[g, x] filled tiles stand at the head of group g's slots for expert x; in every draw one expert is full in every group.
All inputs are finite; a program needn't handle non-finite values.
Results may differ from the reference program's by a relative error of at most 0.0009.
Values may be sent and summed in bfloat16 or wider, within the bound.
A program may use at most 128 MiB of HBM per device.

```python
import math
import jax
import jax.numpy as jnp
from jax import lax

D = 7168
FF = 1024
TILE = 16
TILES = 8
ITERS = 2
GROUPS = 4
EXPERTS = 4


def draw_momentum(key, part):
    key_rows = jax.random.fold_in(key, 11)
    key_cols = jax.random.fold_in(key, 12)
    key_base = jax.random.fold_in(key, 13)
    row_scale = jnp.exp(jax.random.uniform(key_rows, (EXPERTS, 1, FF), jnp.float32, math.log(0.3), math.log(3.0)))
    col_scale = jnp.exp(jax.random.uniform(key_cols, (EXPERTS, D, 1), jnp.float32, math.log(0.3), math.log(3.0)))
    base = jnp.clip(jax.random.normal(key_base, (EXPERTS, D, FF), jnp.float32), -6.0, 6.0)
    return (base * row_scale * col_scale).astype(jnp.float32)


def draw_filled_tile_count(key, part):
    key_counts = jax.random.fold_in(key, 21)
    key_full = jax.random.fold_in(key, 22)
    key_low = jax.random.fold_in(key, 23)
    group_random_key = jax.random.fold_in(key, 24)
    counts = jax.random.randint(key_counts, (GROUPS, EXPERTS), 1, TILES + 1)
    full_expert = jax.random.randint(key_full, (), 0, EXPERTS)
    low_expert = (full_expert + 1 + jax.random.randint(key_low, (), 0, EXPERTS - 1)) % EXPERTS
    low_group = jax.random.randint(group_random_key, (), 0, GROUPS)
    expert_iota = lax.broadcasted_iota(jnp.int32, (GROUPS, EXPERTS), 1)
    group_iota = lax.broadcasted_iota(jnp.int32, (GROUPS, EXPERTS), 0)
    counts = jnp.where(expert_iota == full_expert, TILES, counts)
    counts = jnp.where((expert_iota == low_expert) & (group_iota == low_group), 1, counts)
    return counts.astype(jnp.int32)


def raised(drawn, own_key, source, target, blocks, factor):
    def block_of(axis_at):
        return (jnp.arange(drawn.shape[axis_at]) // (drawn.shape[axis_at] // blocks)).reshape((-1,) + (1,) * (drawn.ndim - 1 - axis_at))

    first = jax.random.permutation(own_key, blocks)[block_of(target)]
    far = (block_of(target) + blocks // 2) % blocks
    return jnp.where((block_of(source) == first) | (block_of(source) == far), factor * drawn, drawn)


def block_scale(stream_key, dims, shards, smallest, top_value):
    level = 1.0
    for dim, shards_of in shards:
        heights = jax.random.uniform(jax.random.fold_in(jax.random.fold_in(stream_key, 6), dim), (shards_of,), jnp.float32, smallest / len(shards), top_value / len(shards))
        level = level * jnp.repeat(jnp.exp(heights), dims[dim] // shards_of).reshape((-1,) + (1,) * (len(dims) - 1 - dim))
    return level


def scatter_about(key, shape, scale, limit, shards=(), held_as=jnp.bfloat16):
    array = scale * jax.random.normal(key, shape, jnp.float32)
    if shards:
        array = array * block_scale(key, shape, shards, -0.22, 0.18)
    return jnp.clip(array, -limit, limit).astype(held_as)


def noise_with(rng, shape, spread, bound, shards, heavy, kind=jnp.bfloat16):
    result = spread * jax.random.normal(rng, shape, jnp.float32)
    if shards:
        result = result * block_scale(rng, shape, shards, -0.22, 0.18)
    return jnp.clip(raised(result, jax.random.fold_in(rng, 3), *heavy), -bound, bound).astype(kind)


def setup_inputs(seed: int = 0) -> dict:
    streams_of = jax.random.split(jax.random.key(seed), 5)
    return {
        "hidden_token_tiles": scatter_about(streams_of[0], (EXPERTS, GROUPS * TILES * TILE, FF), 1.0, 6.0, ((1, 4),)),
        "gradient_token_tiles": noise_with(streams_of[1], (EXPERTS, D, GROUPS * TILES * TILE), 0.1, 0.59765625, ((1, 8), (2, 4)), (2, 0, 4, 2.0)),
        "momentum": draw_momentum(jax.random.fold_in(streams_of[4], 71), 0),
        "filled_tile_count": draw_filled_tile_count(jax.random.fold_in(streams_of[4], 71), 0),
    }


MOMENTUM_DECAY = 0.95
EPSILON = 1e-07
COEF_A = 3.4445
COEF_B = -4.775
COEF_C = 2.0315

def full_dot(left, right):
    return jnp.dot(left, right, precision=lax.Precision.HIGHEST, preferred_element_type=jnp.float32)

def reference(hidden_token_tiles, gradient_token_tiles, momentum, filled_tile_count):
    rows_group = TILES * TILE
    positions = jnp.arange(GROUPS * rows_group, dtype=jnp.int32)
    group_of_rows = positions // rows_group
    within = positions % rows_group
    factor = math.sqrt(max(FF, D))

    def one_expert(index):
        limits = filled_tile_count[:, index] * TILE
        tallied_tiles = within < limits[group_of_rows]
        retained_entries = jnp.where(tallied_tiles[:, None], hidden_token_tiles[index], jnp.zeros((), jnp.bfloat16))
        gradient = jnp.dot(gradient_token_tiles[index], retained_entries, preferred_element_type=jnp.float32)
        moment = MOMENTUM_DECAY * momentum[index] + gradient
        length = jnp.sqrt(jnp.sum(moment * moment))
        current = moment / (length + EPSILON)
        for iteration in range(ITERS):
            gram_matrix = full_dot(current.T, current)
            mixer = COEF_B * gram_matrix + COEF_C * full_dot(gram_matrix, gram_matrix)
            current = COEF_A * current + full_dot(current, mixer)
        return (moment, current * factor)
    moments, muon_updates = lax.map(one_expert, jnp.arange(EXPERTS, dtype=jnp.int32))
    return (moments, muon_updates)
```

```python
import math

import jax
import jax.numpy as jnp
from jax import lax
from jax.sharding import PartitionSpec as P

D = 7168
FF = 1024
TILE = 16
ITERS = 2


MOMENTUM_DECAY = 0.95
EPSILON = 1e-07
COEF_A = 3.4445
COEF_B = -4.775
COEF_C = 2.0315

BF16 = jnp.bfloat16


def dot16(left, right):
    return jnp.dot(left.astype(BF16), right.astype(BF16), preferred_element_type=jnp.float32)


def split16(array):
    high = array.astype(BF16)
    return high, (array - high.astype(jnp.float32)).astype(BF16)


def gram_of(moment):
    high, low = split16(moment)
    cross = jnp.dot(high.T, low, preferred_element_type=jnp.float32)
    return jnp.dot(high.T, high, preferred_element_type=jnp.float32) + cross + cross.T


def mixers(gram):
    first = COEF_B * gram + COEF_C * dot16(gram, gram)
    square = 2.0 * COEF_A * first + dot16(first, first)
    gram_next = COEF_A * COEF_A * gram + dot16(gram, square)
    second = COEF_B * gram_next + COEF_C * dot16(gram_next, gram_next)
    return COEF_A * (first + second) + dot16(first, second)


def body(hidden_token_tiles, gradient_token_tiles, momentum, filled_tile_count):
    group = lax.axis_index("dp")
    rows_group = hidden_token_tiles.shape[1]
    experts_here = hidden_token_tiles.shape[0]
    limits = lax.dynamic_index_in_dim(filled_tile_count, group, 0, keepdims=False) * TILE
    positions = lax.broadcasted_iota(jnp.int32, (experts_here, rows_group), 1)
    tallied_tiles = positions < limits[:, None]
    retained_entries = jnp.where(
        tallied_tiles[:, :, None], hidden_token_tiles, jnp.zeros((), jnp.bfloat16)
    )
    rows_all = lax.all_to_all(retained_entries, "dp", 0, 1, tiled=True)[0]
    columns_all = lax.all_to_all(gradient_token_tiles, "dp", 0, 2, tiled=True)[0]
    gradient = jnp.dot(columns_all, rows_all, preferred_element_type=jnp.float32)
    moment = MOMENTUM_DECAY * momentum[0] + gradient
    gram_total = lax.psum(gram_of(moment).astype(BF16), "expert").astype(jnp.float32)
    factor = 1.0 / (jnp.sqrt(jnp.trace(gram_total)) + EPSILON)
    current = moment * factor
    mixer = mixers(gram_total * (factor * factor))
    current = COEF_A * COEF_A * current + jnp.dot(
        current, mixer, precision=lax.Precision.HIGH, preferred_element_type=jnp.float32
    )
    update_local = current * math.sqrt(max(FF, D))
    gathered = lax.all_gather(update_local.astype(jnp.float16)[None], "dp", axis=0, tiled=True)
    return (moment[None], gathered.astype(jnp.float32))


def solution(mesh):
    placed = (P(None, "dp", None), P(None, "expert", "dp"), P("dp", "expert", None), P())
    return jax.shard_map(
        body,
        mesh=mesh,
        in_specs=placed,
        out_specs=(P("dp", "expert", None), P(None, "expert", None)),
        check_vma=False,
    )
```

```python
import functools
import math

import jax
import jax.numpy as jnp
from jax import lax
from jax.experimental import pallas as pl
from jax.experimental.pallas import tpu as pltpu
from jax.sharding import PartitionSpec as P

D = 7168
FF = 1024
TILE = 16
ITERS = 2


MOMENTUM_DECAY = 0.95
EPSILON = 1e-07
COEF_A = 3.4445
COEF_B = -4.775
COEF_C = 2.0315

BF16 = jnp.bfloat16
OUT = jnp.float32
MESH = pl.DeviceIdType.MESH


BLOCK = 256
PAIR = 2
CHUNKS = 5


def dot16(left, right):
    return jnp.dot(left, right, preferred_element_type=jnp.float32)


def across(left, right):
    return lax.dot_general(left, right, (((0,), (0,)), ((), ())), preferred_element_type=jnp.float32)


def iterate_kernel(
    n, scale, moment_ref, out_ref, high, low, work, near, part, far, done, full,
    gram, gram16, first, first16, second16, other, mix, mix_low,
    near_sem, far_sem, done_sem, full_sem,
):
    me = lax.axis_index("expert")
    half, place = lax.rem(me, PAIR), lax.div(me, PAIR)
    places = n // PAIR
    piece = BLOCK // places
    partner = me + 1 - 2 * half
    size = moment_ref.shape[1]
    blocks = size // BLOCK
    pairs = [(i, j) for i in range(blocks) for j in range(i, blocks)]

    def peer(offset):
        return lax.rem(place + offset, places)

    def device(at):
        return {"expert": at}

    barrier = pltpu.get_barrier_semaphore()
    pl.semaphore_signal(barrier, inc=1, device_id=device(partner), device_id_type=MESH)
    for offset in range(1, places):
        pl.semaphore_signal(
            barrier, inc=1, device_id=device(peer(offset) * PAIR + half), device_id_type=MESH
        )

    sends = []

    def send(source, target, sems, at, to):
        copy = pltpu.make_async_remote_copy(
            src_ref=source,
            dst_ref=target,
            send_sem=sems.at[(0, *at)],
            recv_sem=sems.at[(1, *at)],
            device_id=device(to),
            device_id_type=MESH,
        )
        copy.start()
        sends.append(copy)
        return copy

    near_copies, far_copies, done_copies, full_copies = {}, {}, {}, {}

    def send_near(chunk):
        near_copies[chunk] = send(
            work.at[chunk, 1 - half], near.at[chunk], near_sem, (chunk,), partner
        )

    def send_far(chunk):
        near_copies[chunk].wait_recv()
        total = work[chunk, half].astype(jnp.float32) + near[chunk].astype(jnp.float32)
        part[chunk] = total.astype(BF16)
        for offset in range(1, places):
            to = peer(offset)
            rows = pl.ds(pl.multiple_of(to * piece, piece), piece)
            far_copies[chunk, offset] = send(
                part.at[chunk, rows],
                far.at[chunk, offset],
                far_sem,
                (chunk, offset),
                to * PAIR + half,
            )

    def send_done(chunk):
        mine = pl.ds(pl.multiple_of(place * piece, piece), piece)
        total = part[chunk, mine].astype(jnp.float32)
        for offset in range(1, places):
            far_copies[chunk, offset].wait_recv()
            total = total + far[chunk, offset].astype(jnp.float32)
        done[chunk] = total.astype(BF16)
        full[chunk, half, mine] = total.astype(BF16)
        for offset in range(1, places):
            done_copies[chunk, offset] = send(
                done.at[chunk],
                full.at[chunk, half, mine],
                done_sem,
                (chunk, offset),
                peer(offset) * PAIR + half,
            )

    def wait_done(chunk):
        for offset in range(1, places):
            source = lax.rem(place + places - offset, places)
            rows = pl.ds(pl.multiple_of(source * piece, piece), piece)
            pltpu.make_async_remote_copy(
                src_ref=done.at[chunk],
                dst_ref=full.at[chunk, half, rows],
                send_sem=done_sem.at[0, chunk, offset],
                recv_sem=done_sem.at[1, chunk, offset],
                device_id=device(partner),
                device_id_type=MESH,
            ).wait_recv()

    def send_full(chunk):
        wait_done(chunk)
        full_copies[chunk] = send(
            full.at[chunk, half], full.at[chunk, half], full_sem, (chunk,), partner
        )

    moment = moment_ref[...]
    rounded = moment.astype(BF16)
    high[...] = rounded
    low[...] = (moment - rounded.astype(jnp.float32)).astype(BF16)
    at = 0
    for i in range(blocks):
        rows = slice(i * BLOCK, (i + 1) * BLOCK)
        rest = slice(i * BLOCK, size)
        strip = across(high[:, rows], high[:, rest])
        strip += across(high[:, rows], low[:, rest]) + across(low[:, rows], high[:, rest])
        for j in range(i, blocks):
            block = strip[:, (j - i) * BLOCK : (j - i + 1) * BLOCK]
            work[at // PAIR, at % PAIR] = block.astype(BF16)
            at += 1
        if i == 0:
            pl.semaphore_wait(barrier, places)
        for chunk in range(len(near_copies), at // PAIR):
            send_near(chunk)
    for step in range(CHUNKS + 2):
        if step < CHUNKS:
            send_far(step)
        if 0 <= step - 1 < CHUNKS:
            send_done(step - 1)
        if 0 <= step - 2:
            send_full(step - 2)
    for chunk in range(CHUNKS):
        pltpu.make_async_remote_copy(
            src_ref=full.at[chunk, half],
            dst_ref=full.at[chunk, 1 - half],
            send_sem=full_sem.at[0, chunk],
            recv_sem=full_sem.at[1, chunk],
            device_id=device(partner),
            device_id_type=MESH,
        ).wait_recv()
    for copy in sends:
        copy.wait_send()

    trace = jnp.zeros((1, 1), jnp.float32)
    row_at = lax.broadcasted_iota(jnp.int32, (BLOCK, BLOCK), 0)
    col_at = lax.broadcasted_iota(jnp.int32, (BLOCK, BLOCK), 1)
    for at, (i, j) in enumerate(pairs):
        block = full[at // PAIR, at % PAIR].astype(jnp.float32)
        if i == j:
            trace += jnp.sum(jnp.where(row_at == col_at, block, 0.0), keepdims=True)
        gram[i * BLOCK : (i + 1) * BLOCK, j * BLOCK : (j + 1) * BLOCK] = block
        if i != j:
            gram[j * BLOCK : (j + 1) * BLOCK, i * BLOCK : (i + 1) * BLOCK] = block.T
    factor = 1.0 / (jnp.sqrt(trace) + EPSILON)

    def strips(step):
        @pl.loop(0, blocks)
        def _(i):
            step(pl.ds(pl.multiple_of(i * BLOCK, BLOCK), BLOCK))

    def scaled(rows):
        value = gram[rows] * (factor * factor)
        gram[rows] = value
        gram16[rows] = value.astype(BF16)

    def mix_first(rows):
        value = COEF_B * gram[rows] + COEF_C * dot16(gram16[rows], gram16[...])
        first[rows] = value
        first16[rows] = value.astype(BF16)

    def mix_square(rows):
        value = 2.0 * COEF_A * first[rows] + dot16(first16[rows], first16[...])
        other[rows] = value.astype(BF16)

    def next_gram(rows):
        value = COEF_A * COEF_A * gram[rows] + dot16(gram16[rows], other[...])
        gram[rows] = value
        mix[rows] = value.astype(BF16)

    def mix_second(rows):
        value = COEF_B * gram[rows] + COEF_C * dot16(mix[rows], mix[...])
        gram[rows] = value
        second16[rows] = value.astype(BF16)

    def mix_both(rows):
        value = COEF_A * (first[rows] + gram[rows]) + dot16(first16[rows], second16[...])
        top = value.astype(BF16)
        gram16[rows] = top
        mix_low[rows] = (value - top.astype(jnp.float32)).astype(BF16)

    for step in (scaled, mix_first, mix_square, next_gram, mix_second, mix_both):
        strips(step)

    tall = moment_ref.shape[0]
    stride = math.gcd(tall, 128)

    @pl.loop(0, tall // stride)
    def _(i):
        rows = pl.ds(pl.multiple_of(i * stride, stride), stride)
        value = dot16(high[rows], gram16[...]) + dot16(low[rows], gram16[...])
        value += dot16(high[rows], mix_low[...]) + COEF_A * COEF_A * moment_ref[rows]
        out_ref[rows] = (value * (factor * scale)).astype(out_ref.dtype)


def iterated(moment, n):
    tall, size = moment.shape
    square = (size, size)
    places = n // PAIR
    piece = BLOCK // places
    vmem, dma = pltpu.VMEM, pltpu.SemaphoreType.DMA
    scratch = [vmem((tall, size), BF16)] * 2 + [
        vmem((CHUNKS, PAIR, BLOCK, BLOCK), BF16),
        vmem((CHUNKS, BLOCK, BLOCK), BF16),
        vmem((CHUNKS, BLOCK, BLOCK), BF16),
        vmem((CHUNKS, places, piece, BLOCK), BF16),
        vmem((CHUNKS, piece, BLOCK), BF16),
        vmem((CHUNKS, PAIR, BLOCK, BLOCK), BF16),
        vmem(square, jnp.float32),
        vmem(square, BF16),
        vmem(square, jnp.float32),
        vmem(square, BF16),
        vmem(square, BF16),
        vmem(square, BF16),
        vmem(square, BF16),
        vmem(square, BF16),
        dma((2, CHUNKS)),
        dma((2, CHUNKS, places)),
        dma((2, CHUNKS, places)),
        dma((2, CHUNKS)),
    ]
    return pl.pallas_call(
        functools.partial(iterate_kernel, n, math.sqrt(max(FF, D))),
        out_shape=jax.ShapeDtypeStruct(moment.shape, OUT),
        in_specs=[pl.BlockSpec(memory_space=pltpu.VMEM)],
        out_specs=pl.BlockSpec(memory_space=pltpu.VMEM),
        scratch_shapes=scratch,
        compiler_params=pltpu.CompilerParams(
            collective_id=0, has_side_effects=True, vmem_limit_bytes=56 * 2**20
        ),
    )(moment)


def body(hidden_token_tiles, gradient_token_tiles, momentum, filled_tile_count):
    group = lax.axis_index("dp")
    rows_group = hidden_token_tiles.shape[1]
    experts_here = hidden_token_tiles.shape[0]
    limits = lax.dynamic_index_in_dim(filled_tile_count, group, 0, keepdims=False) * TILE
    positions = lax.broadcasted_iota(jnp.int32, (experts_here, rows_group), 1)
    tallied_tiles = positions < limits[:, None]
    retained_entries = jnp.where(
        tallied_tiles[:, :, None], hidden_token_tiles, jnp.zeros((), jnp.bfloat16)
    )
    rows_all = lax.all_to_all(retained_entries, "dp", 0, 1, tiled=True)[0]
    columns_all = lax.all_to_all(gradient_token_tiles, "dp", 0, 2, tiled=True)[0]
    gradient = jnp.dot(columns_all, rows_all, preferred_element_type=jnp.float32)
    moment = MOMENTUM_DECAY * momentum[0] + gradient
    update_local = iterated(moment, lax.axis_size("expert"))
    gathered = lax.all_gather(update_local.astype(jnp.float16)[None], "dp", axis=0, tiled=True)
    return (moment[None], gathered.astype(jnp.float32))


def solution(mesh):
    placed = (P(None, "dp", None), P(None, "expert", "dp"), P("dp", "expert", None), P())
    return jax.shard_map(
        body,
        mesh=mesh,
        in_specs=placed,
        out_specs=(P("dp", "expert", None), P(None, "expert", None)),
        check_vma=False,
    )
```

```python
import functools
import math

import jax
import jax.numpy as jnp
from jax import lax
from jax.experimental import pallas as pl
from jax.experimental.pallas import tpu as pltpu
from jax.sharding import PartitionSpec as P

D = 7168
FF = 1024
TILE = 16
ITERS = 2


MOMENTUM_DECAY = 0.95
EPSILON = 1e-07
COEF_A = 3.4445
COEF_B = -4.775
COEF_C = 2.0315

BF16 = jnp.bfloat16
LEVELS = 32700.0
MESH = pl.DeviceIdType.MESH


BLOCK = 256
PAIR = 2
CHUNKS = 5


def dot16(left, right):
    return jnp.dot(left, right, preferred_element_type=jnp.float32)


def across(left, right):
    return lax.dot_general(left, right, (((0,), (0,)), ((), ())), preferred_element_type=jnp.float32)


def iterate_kernel(
    n, groups, scale, moment_ref, code_ref, top_ref, high, low, work, near, part, far, done, full,
    gram, gram16, first, first16, second16, other, mix, mix_low, code, top,
    near_sem, far_sem, done_sem, full_sem, twin_sem, group_sem, pass_sem, top_sem, local_sem,
):
    me = lax.axis_index("expert")
    group = lax.axis_index("dp")
    twin = group + 1 - 2 * lax.rem(group, PAIR)
    half, place = lax.rem(me, PAIR), lax.div(me, PAIR)
    places = n // PAIR
    piece = BLOCK // places
    partner = me + 1 - 2 * half
    size = moment_ref.shape[1]
    blocks = size // BLOCK
    pairs = [(i, j) for i in range(blocks) for j in range(i, blocks)]

    def peer(offset):
        return lax.rem(place + offset, places)

    def device(at):
        return {"expert": at}

    barrier = pltpu.get_barrier_semaphore()
    pl.semaphore_signal(barrier, inc=1, device_id=device(partner), device_id_type=MESH)
    for offset in range(1, places):
        pl.semaphore_signal(
            barrier, inc=1, device_id=device(peer(offset) * PAIR + half), device_id_type=MESH
        )

    for offset in range(1, groups):
        pl.semaphore_signal(
            barrier,
            inc=1,
            device_id={"dp": lax.rem(group + offset, groups)},
            device_id_type=MESH,
        )

    sends = []

    def send(source, target, sems, at, to):
        copy = pltpu.make_async_remote_copy(
            src_ref=source,
            dst_ref=target,
            send_sem=sems.at[(0, *at)],
            recv_sem=sems.at[(1, *at)],
            device_id=to if isinstance(to, dict) else device(to),
            device_id_type=MESH,
        )
        copy.start()
        sends.append(copy)
        return copy

    near_copies, far_copies, done_copies, full_copies = {}, {}, {}, {}

    def send_near(chunk):
        near_copies[chunk] = send(
            work.at[chunk, 1 - half], near.at[chunk], near_sem, (chunk,), partner
        )

    def send_far(chunk):
        near_copies[chunk].wait_recv()
        total = work[chunk, half].astype(jnp.float32) + near[chunk].astype(jnp.float32)
        part[chunk] = total.astype(BF16)
        for offset in range(1, places):
            to = peer(offset)
            rows = pl.ds(pl.multiple_of(to * piece, piece), piece)
            far_copies[chunk, offset] = send(
                part.at[chunk, rows],
                far.at[chunk, offset],
                far_sem,
                (chunk, offset),
                to * PAIR + half,
            )

    def send_done(chunk):
        mine = pl.ds(pl.multiple_of(place * piece, piece), piece)
        total = part[chunk, mine].astype(jnp.float32)
        for offset in range(1, places):
            far_copies[chunk, offset].wait_recv()
            total = total + far[chunk, offset].astype(jnp.float32)
        done[chunk] = total.astype(BF16)
        full[chunk, half, mine] = total.astype(BF16)
        for offset in range(1, places):
            done_copies[chunk, offset] = send(
                done.at[chunk],
                full.at[chunk, half, mine],
                done_sem,
                (chunk, offset),
                peer(offset) * PAIR + half,
            )

    def wait_done(chunk):
        for offset in range(1, places):
            source = lax.rem(place + places - offset, places)
            rows = pl.ds(pl.multiple_of(source * piece, piece), piece)
            pltpu.make_async_remote_copy(
                src_ref=done.at[chunk],
                dst_ref=full.at[chunk, half, rows],
                send_sem=done_sem.at[0, chunk, offset],
                recv_sem=done_sem.at[1, chunk, offset],
                device_id=device(partner),
                device_id_type=MESH,
            ).wait_recv()

    def send_full(chunk):
        wait_done(chunk)
        full_copies[chunk] = send(
            full.at[chunk, half], full.at[chunk, half], full_sem, (chunk,), partner
        )

    moment = moment_ref[...]
    rounded = moment.astype(BF16)
    high[...] = rounded
    low[...] = (moment - rounded.astype(jnp.float32)).astype(BF16)
    at = 0
    for i in range(blocks):
        rows = slice(i * BLOCK, (i + 1) * BLOCK)
        rest = slice(i * BLOCK, size)
        strip = across(high[:, rows], high[:, rest])
        strip += across(high[:, rows], low[:, rest]) + across(low[:, rows], high[:, rest])
        for j in range(i, blocks):
            block = strip[:, (j - i) * BLOCK : (j - i + 1) * BLOCK]
            work[at // PAIR, at % PAIR] = block.astype(BF16)
            at += 1
        if i == 0:
            pl.semaphore_wait(barrier, places + groups - 1)
        for chunk in range(len(near_copies), at // PAIR):
            send_near(chunk)
    for step in range(CHUNKS + 2):
        if step < CHUNKS:
            send_far(step)
        if 0 <= step - 1 < CHUNKS:
            send_done(step - 1)
        if 0 <= step - 2:
            send_full(step - 2)
    for chunk in range(CHUNKS):
        pltpu.make_async_remote_copy(
            src_ref=full.at[chunk, half],
            dst_ref=full.at[chunk, 1 - half],
            send_sem=full_sem.at[0, chunk],
            recv_sem=full_sem.at[1, chunk],
            device_id=device(partner),
            device_id_type=MESH,
        ).wait_recv()
    trace = jnp.zeros((1, 1), jnp.float32)
    row_at = lax.broadcasted_iota(jnp.int32, (BLOCK, BLOCK), 0)
    col_at = lax.broadcasted_iota(jnp.int32, (BLOCK, BLOCK), 1)
    for at, (i, j) in enumerate(pairs):
        block = full[at // PAIR, at % PAIR].astype(jnp.float32)
        if i == j:
            trace += jnp.sum(jnp.where(row_at == col_at, block, 0.0), keepdims=True)
        gram[i * BLOCK : (i + 1) * BLOCK, j * BLOCK : (j + 1) * BLOCK] = block
        if i != j:
            gram[j * BLOCK : (j + 1) * BLOCK, i * BLOCK : (i + 1) * BLOCK] = block.T
    factor = 1.0 / (jnp.sqrt(trace) + EPSILON)

    def strips(step):
        @pl.loop(0, blocks)
        def _(i):
            step(pl.ds(pl.multiple_of(i * BLOCK, BLOCK), BLOCK))

    def scaled(rows):
        value = gram[rows] * (factor * factor)
        gram[rows] = value
        gram16[rows] = value.astype(BF16)

    def mix_first(rows):
        value = COEF_B * gram[rows] + COEF_C * dot16(gram16[rows], gram16[...])
        first[rows] = value
        first16[rows] = value.astype(BF16)

    def mix_square(rows):
        value = 2.0 * COEF_A * first[rows] + dot16(first16[rows], first16[...])
        other[rows] = value.astype(BF16)

    def next_gram(rows):
        value = COEF_A * COEF_A * gram[rows] + dot16(gram16[rows], other[...])
        gram[rows] = value
        mix[rows] = value.astype(BF16)

    def mix_second(rows):
        value = COEF_B * gram[rows] + COEF_C * dot16(mix[rows], mix[...])
        gram[rows] = value
        second16[rows] = value.astype(BF16)

    def mix_both(rows):
        value = COEF_A * (first[rows] + gram[rows]) + dot16(first16[rows], second16[...])
        top = value.astype(BF16)
        gram16[rows] = top
        mix_low[rows] = (value - top.astype(jnp.float32)).astype(BF16)

    for step in (scaled, mix_first, mix_square, next_gram, mix_second, mix_both):
        strips(step)

    stride = code.shape[1]
    parts = code.shape[0]
    locals_ = []
    group_copies = {}
    top[...] = jnp.zeros_like(top)
    for i in range(parts):
        rows = slice(i * stride, (i + 1) * stride)
        value = dot16(high[rows], gram16[...]) + dot16(low[rows], gram16[...])
        value += dot16(high[rows], mix_low[...]) + COEF_A * COEF_A * moment_ref[rows]
        value = value * (factor * scale)
        peak = jnp.maximum(jnp.max(jnp.abs(value), axis=0, keepdims=True), 1e-30)
        top[i : i + 1] = peak * (1.0 / LEVELS)
        code[i] = jnp.round(value * (LEVELS / peak)).astype(jnp.int32).astype(jnp.int16)
        place_here = code_ref.at[group, i]
        for offset in range(1, groups // PAIR):
            to = {"dp": lax.rem(group + PAIR * offset, groups)}
            group_copies[i, offset] = send(code.at[i], place_here, group_sem, (i, offset), to)
        send(code.at[i], place_here, twin_sem, (i,), {"dp": twin})
        copy = pltpu.make_async_copy(code.at[i], place_here, local_sem.at[i])
        copy.start()
        locals_.append(copy)
    for offset in range(1, groups):
        to = {"dp": lax.rem(group + offset, groups)}
        send(top, top_ref.at[group], top_sem, (offset,), to)
    copy = pltpu.make_async_copy(top, top_ref.at[group], local_sem.at[parts])
    copy.start()
    locals_.append(copy)

    def arrival(target, sems, at):
        pltpu.make_async_remote_copy(
            src_ref=target,
            dst_ref=target,
            send_sem=sems.at[(0, *at)],
            recv_sem=sems.at[(1, *at)],
            device_id={"dp": twin},
            device_id_type=MESH,
        ).wait_recv()

    for i in range(parts):
        for offset in range(1, groups // PAIR):
            source = lax.rem(group + groups - PAIR * offset, groups)
            there = code_ref.at[source, i]
            arrival(there, group_sem, (i, offset))
            send(there, there, pass_sem, (i, offset), {"dp": twin})
    for i in range(parts):
        arrival(code_ref.at[twin, i], twin_sem, (i,))
        for offset in range(1, groups // PAIR):
            source = lax.rem(twin + groups - PAIR * offset, groups)
            arrival(code_ref.at[source, i], pass_sem, (i, offset))
    for offset in range(1, groups):
        source = lax.rem(group + groups - offset, groups)
        arrival(top_ref.at[source], top_sem, (offset,))
    for copy in sends:
        copy.wait_send()
    for copy in locals_:
        copy.wait()


def iterated(moment, n, groups):
    tall, size = moment.shape
    square = (size, size)
    places = n // PAIR
    piece = BLOCK // places
    stride = math.gcd(tall, 128)
    parts = tall // stride
    tops = -(-parts // 8) * 8
    links = groups // PAIR
    vmem, dma = pltpu.VMEM, pltpu.SemaphoreType.DMA
    scratch = [vmem((tall, size), BF16)] * 2 + [
        vmem((CHUNKS, PAIR, BLOCK, BLOCK), BF16),
        vmem((CHUNKS, BLOCK, BLOCK), BF16),
        vmem((CHUNKS, BLOCK, BLOCK), BF16),
        vmem((CHUNKS, places, piece, BLOCK), BF16),
        vmem((CHUNKS, piece, BLOCK), BF16),
        vmem((CHUNKS, PAIR, BLOCK, BLOCK), BF16),
        vmem(square, jnp.float32),
        vmem(square, BF16),
        vmem(square, jnp.float32),
        vmem(square, BF16),
        vmem(square, BF16),
        vmem(square, BF16),
        vmem(square, BF16),
        vmem(square, BF16),
        vmem((parts, stride, size), jnp.int16),
        vmem((tops, size), jnp.float32),
        dma((2, CHUNKS)),
        dma((2, CHUNKS, places)),
        dma((2, CHUNKS, places)),
        dma((2, CHUNKS)),
        dma((2, parts)),
        dma((2, parts, links)),
        dma((2, parts, links)),
        dma((2, groups)),
        dma((parts + 1,)),
    ]
    code, top = pl.pallas_call(
        functools.partial(iterate_kernel, n, groups, math.sqrt(max(FF, D))),
        out_shape=(
            jax.ShapeDtypeStruct((groups, parts, stride, size), jnp.int16),
            jax.ShapeDtypeStruct((groups, tops, size), jnp.float32),
        ),
        in_specs=[pl.BlockSpec(memory_space=pltpu.VMEM)],
        out_specs=(pl.BlockSpec(memory_space=pl.ANY),) * 2,
        scratch_shapes=scratch,
        compiler_params=pltpu.CompilerParams(
            collective_id=0, has_side_effects=True, vmem_limit_bytes=56 * 2**20
        ),
    )(moment)
    update = code.astype(jnp.float32) * top[:, :parts, None]
    return update.reshape(groups, tall, size)


def body(hidden_token_tiles, gradient_token_tiles, momentum, filled_tile_count):
    group = lax.axis_index("dp")
    rows_group = hidden_token_tiles.shape[1]
    experts_here = hidden_token_tiles.shape[0]
    limits = lax.dynamic_index_in_dim(filled_tile_count, group, 0, keepdims=False) * TILE
    positions = lax.broadcasted_iota(jnp.int32, (experts_here, rows_group), 1)
    tallied_tiles = positions < limits[:, None]
    retained_entries = jnp.where(
        tallied_tiles[:, :, None], hidden_token_tiles, jnp.zeros((), jnp.bfloat16)
    )
    rows_all = lax.all_to_all(retained_entries, "dp", 0, 1, tiled=True)[0]
    columns_all = lax.all_to_all(gradient_token_tiles, "dp", 0, 2, tiled=True)[0]
    gradient = jnp.dot(columns_all, rows_all, preferred_element_type=jnp.float32)
    moment = MOMENTUM_DECAY * momentum[0] + gradient
    update = iterated(moment, lax.axis_size("expert"), lax.axis_size("dp"))
    return (moment[None], update)


def solution(mesh):
    placed = (P(None, "dp", None), P(None, "expert", "dp"), P("dp", "expert", None), P())
    return jax.shard_map(
        body,
        mesh=mesh,
        in_specs=placed,
        out_specs=(P("dp", "expert", None), P(None, "expert", None)),
        check_vma=False,
    )
```

```python
import functools
import math

import jax
import jax.numpy as jnp
from jax import lax
from jax.experimental import pallas as pl
from jax.experimental.pallas import tpu as pltpu
from jax.sharding import PartitionSpec as P

D = 7168
FF = 1024
TILE = 16
ITERS = 2


MOMENTUM_DECAY = 0.95
EPSILON = 1e-07
COEF_A = 3.4445
COEF_B = -4.775
COEF_C = 2.0315

BF16 = jnp.bfloat16
LEVELS = 32700.0
MESH = pl.DeviceIdType.MESH


BLOCK = 256
PAIR = 2
TEAM = 4
CHUNKS = 5


def dot16(left, right):
    return jnp.dot(left, right, preferred_element_type=jnp.float32)


def across(left, right):
    return lax.dot_general(left, right, (((0,), (0,)), ((), ())), preferred_element_type=jnp.float32)


def exchange_kernel(
    n, groups, tiles_ref, hidden_ref, columns_ref, rows_ref,
    twin_sem, tile_sem, piece_sem, pass_sem, local_sem,
):
    me = lax.axis_index("expert")
    group = lax.axis_index("dp")
    twin = group + 1 - 2 * lax.rem(group, PAIR)
    member = lax.rem(me, TEAM)
    team = me - member
    deep = hidden_ref.shape[1]
    piece = deep // TEAM
    hops = range(1, groups // PAIR)

    barrier = pltpu.get_barrier_semaphore()
    for offset in range(1, groups):
        to = {"dp": lax.rem(group + offset, groups)}
        pl.semaphore_signal(barrier, inc=1, device_id=to, device_id_type=MESH)
    for offset in range(1, TEAM):
        to = {"expert": team + lax.rem(member + offset, TEAM)}
        pl.semaphore_signal(barrier, inc=1, device_id=to, device_id_type=MESH)

    def slot(at):
        return columns_ref.at[:, pl.ds(pl.multiple_of(at * deep, deep), deep)]

    def strip(ref, at, which):
        return ref.at[at, pl.ds(pl.multiple_of(which * piece, piece), piece)]

    local = [
        pltpu.make_async_copy(hidden_ref.at[group], rows_ref.at[group], local_sem.at[0]),
        pltpu.make_async_copy(tiles_ref.at[group], slot(group), local_sem.at[1]),
    ]
    for copy in local:
        copy.start()
    pl.semaphore_wait(barrier, groups - 1 + TEAM - 1)

    def copy_of(source, target, sems, at, to):
        return pltpu.make_async_remote_copy(
            src_ref=source,
            dst_ref=target,
            send_sem=sems.at[(0, *at)],
            recv_sem=sems.at[(1, *at)],
            device_id=to,
            device_id_type=MESH,
        )

    sends, arrivals = [], []

    def send(*copy):
        sends.append(copy_of(*copy))
        sends[-1].start()

    def arrival(target, sems, at):
        return copy_of(target, target, sems, at, {"dp": twin})

    for hop in hops:
        for kind, base in enumerate((group, twin)):
            to = lax.rem(base + PAIR * hop, groups)
            send(
                strip(hidden_ref, to, member), strip(rows_ref, group, member),
                piece_sem, (kind, hop), {"dp": to},
            )
    for hop in hops:
        for kind, base in enumerate((group, twin)):
            to = lax.rem(base + PAIR * hop, groups)
            send(tiles_ref.at[to], slot(group), tile_sem, (kind, hop), {"dp": to})
    send(hidden_ref.at[twin], rows_ref.at[group], twin_sem, (0,), {"dp": twin})
    send(tiles_ref.at[twin], slot(group), twin_sem, (1,), {"dp": twin})
    for hop in hops:
        for kind, base in enumerate((group, twin)):
            source = lax.rem(base + groups - PAIR * hop, groups)
            mine = strip(rows_ref, source, member)
            arrival(mine, piece_sem, (kind, hop)).wait_recv()
            for offset in range(1, TEAM):
                to = {"expert": team + lax.rem(member + offset, TEAM)}
                send(mine, mine, pass_sem, (kind, hop, offset), to)
                other = lax.rem(member + TEAM - offset, TEAM)
                arrivals.append(
                    arrival(strip(rows_ref, source, other), pass_sem, (kind, hop, offset))
                )
            arrivals.append(arrival(slot(source), tile_sem, (kind, hop)))
    arrivals.append(arrival(rows_ref.at[twin], twin_sem, (0,)))
    arrivals.append(arrival(slot(twin), twin_sem, (1,)))
    for copy in arrivals:
        copy.wait_recv()
    for copy in sends:
        copy.wait_send()
    for copy in local:
        copy.wait()


def exchanged(tiles, hidden, n, groups):
    _, tall, deep = tiles.shape
    size = hidden.shape[2]
    hops = groups // PAIR
    dma = pltpu.SemaphoreType.DMA
    return pl.pallas_call(
        functools.partial(exchange_kernel, n, groups),
        out_shape=(
            jax.ShapeDtypeStruct((tall, groups * deep), BF16),
            jax.ShapeDtypeStruct((groups, deep, size), BF16),
        ),
        in_specs=[pl.BlockSpec(memory_space=pl.ANY)] * 2,
        out_specs=(pl.BlockSpec(memory_space=pl.ANY),) * 2,
        scratch_shapes=[
            dma((2, 2)),
            dma((2, 2, hops)),
            dma((2, 2, hops)),
            dma((2, 2, hops, TEAM)),
            dma((2,)),
        ],
        compiler_params=pltpu.CompilerParams(collective_id=1, has_side_effects=True),
    )(tiles, hidden)


def moment_kernel(count_ref, columns_ref, rows_ref, momentum_ref, out_ref, kept):
    group = lax.axis_index("dp")
    groups, deep, size = rows_ref.shape

    @pl.when(pl.program_id(0) == 0)
    def _():
        at = lax.broadcasted_iota(jnp.int32, (deep, size), 0)
        for source in range(groups):
            tallied = at < count_ref[source, group] * TILE
            values = jnp.where(tallied, rows_ref[source].astype(jnp.float32), 0.0)
            kept[source * deep : (source + 1) * deep] = values.astype(BF16)

    gradient = dot16(columns_ref[...], kept[...])
    out_ref[...] = MOMENTUM_DECAY * momentum_ref[...] + gradient


def moment_of(counts, columns, rows, momentum):
    tall, size = momentum.shape
    stride = math.gcd(tall, 128)
    return pl.pallas_call(
        moment_kernel,
        grid=(tall // stride,),
        out_shape=jax.ShapeDtypeStruct(momentum.shape, jnp.float32),
        in_specs=[
            pl.BlockSpec(memory_space=pltpu.SMEM),
            pl.BlockSpec((stride, columns.shape[1]), lambda i: (i, 0)),
            pl.BlockSpec(rows.shape, lambda i: (0, 0, 0)),
            pl.BlockSpec((stride, size), lambda i: (i, 0)),
        ],
        out_specs=pl.BlockSpec((stride, size), lambda i: (i, 0)),
        scratch_shapes=[pltpu.VMEM((columns.shape[1], size), BF16)],
        compiler_params=pltpu.CompilerParams(vmem_limit_bytes=56 * 2**20),
    )(counts, columns, rows, momentum)


def widen_kernel(code_ref, top_ref, out_ref):
    for i in range(code_ref.shape[1]):
        stride = code_ref.shape[2]
        rows = slice(i * stride, (i + 1) * stride)
        out_ref[0, rows] = code_ref[0, i].astype(jnp.float32) * top_ref[0, i : i + 1]


def widened(code, top):
    groups, parts, stride, size = code.shape
    return pl.pallas_call(
        widen_kernel,
        grid=(groups,),
        out_shape=jax.ShapeDtypeStruct((groups, parts * stride, size), jnp.float32),
        in_specs=[
            pl.BlockSpec((1, parts, stride, size), lambda i: (i, 0, 0, 0)),
            pl.BlockSpec((1, top.shape[1], size), lambda i: (i, 0, 0)),
        ],
        out_specs=pl.BlockSpec((1, parts * stride, size), lambda i: (i, 0, 0)),
        compiler_params=pltpu.CompilerParams(vmem_limit_bytes=56 * 2**20),
    )(code, top)


def iterate_kernel(
    n, groups, scale, moment_ref, code_ref, top_ref, high, low, work, near, part, far, done, full,
    gram, gram16, first, first16, second16, other, mix, mix_low, code, top,
    near_sem, far_sem, done_sem, full_sem, twin_sem, group_sem, pass_sem, top_sem, local_sem,
):
    me = lax.axis_index("expert")
    group = lax.axis_index("dp")
    twin = group + 1 - 2 * lax.rem(group, PAIR)
    half, place = lax.rem(me, PAIR), lax.div(me, PAIR)
    places = n // PAIR
    piece = BLOCK // places
    partner = me + 1 - 2 * half
    size = moment_ref.shape[1]
    blocks = size // BLOCK
    pairs = [(i, j) for i in range(blocks) for j in range(i, blocks)]

    def peer(offset):
        return lax.rem(place + offset, places)

    def device(at):
        return {"expert": at}

    barrier = pltpu.get_barrier_semaphore()
    pl.semaphore_signal(barrier, inc=1, device_id=device(partner), device_id_type=MESH)
    for offset in range(1, places):
        pl.semaphore_signal(
            barrier, inc=1, device_id=device(peer(offset) * PAIR + half), device_id_type=MESH
        )

    for offset in range(1, groups):
        pl.semaphore_signal(
            barrier,
            inc=1,
            device_id={"dp": lax.rem(group + offset, groups)},
            device_id_type=MESH,
        )

    sends = []

    def send(source, target, sems, at, to):
        copy = pltpu.make_async_remote_copy(
            src_ref=source,
            dst_ref=target,
            send_sem=sems.at[(0, *at)],
            recv_sem=sems.at[(1, *at)],
            device_id=to if isinstance(to, dict) else device(to),
            device_id_type=MESH,
        )
        copy.start()
        sends.append(copy)
        return copy

    near_copies, far_copies, done_copies, full_copies = {}, {}, {}, {}

    def send_near(chunk):
        near_copies[chunk] = send(
            work.at[chunk, 1 - half], near.at[chunk], near_sem, (chunk,), partner
        )

    def send_far(chunk):
        near_copies[chunk].wait_recv()
        total = work[chunk, half].astype(jnp.float32) + near[chunk].astype(jnp.float32)
        part[chunk] = total.astype(BF16)
        for offset in range(1, places):
            to = peer(offset)
            rows = pl.ds(pl.multiple_of(to * piece, piece), piece)
            far_copies[chunk, offset] = send(
                part.at[chunk, rows],
                far.at[chunk, offset],
                far_sem,
                (chunk, offset),
                to * PAIR + half,
            )

    def send_done(chunk):
        mine = pl.ds(pl.multiple_of(place * piece, piece), piece)
        total = part[chunk, mine].astype(jnp.float32)
        for offset in range(1, places):
            far_copies[chunk, offset].wait_recv()
            total = total + far[chunk, offset].astype(jnp.float32)
        done[chunk] = total.astype(BF16)
        full[chunk, half, mine] = total.astype(BF16)
        for offset in range(1, places):
            done_copies[chunk, offset] = send(
                done.at[chunk],
                full.at[chunk, half, mine],
                done_sem,
                (chunk, offset),
                peer(offset) * PAIR + half,
            )

    def wait_done(chunk):
        for offset in range(1, places):
            source = lax.rem(place + places - offset, places)
            rows = pl.ds(pl.multiple_of(source * piece, piece), piece)
            pltpu.make_async_remote_copy(
                src_ref=done.at[chunk],
                dst_ref=full.at[chunk, half, rows],
                send_sem=done_sem.at[0, chunk, offset],
                recv_sem=done_sem.at[1, chunk, offset],
                device_id=device(partner),
                device_id_type=MESH,
            ).wait_recv()

    def send_full(chunk):
        wait_done(chunk)
        full_copies[chunk] = send(
            full.at[chunk, half], full.at[chunk, half], full_sem, (chunk,), partner
        )

    moment = moment_ref[...]
    rounded = moment.astype(BF16)
    high[...] = rounded
    low[...] = (moment - rounded.astype(jnp.float32)).astype(BF16)
    at = 0
    for i in range(blocks):
        rows = slice(i * BLOCK, (i + 1) * BLOCK)
        rest = slice(i * BLOCK, size)
        strip = across(high[:, rows], high[:, rest])
        strip += across(high[:, rows], low[:, rest]) + across(low[:, rows], high[:, rest])
        for j in range(i, blocks):
            block = strip[:, (j - i) * BLOCK : (j - i + 1) * BLOCK]
            work[at // PAIR, at % PAIR] = block.astype(BF16)
            at += 1
        if i == 0:
            pl.semaphore_wait(barrier, places + groups - 1)
        for chunk in range(len(near_copies), at // PAIR):
            send_near(chunk)
    for step in range(CHUNKS + 2):
        if step < CHUNKS:
            send_far(step)
        if 0 <= step - 1 < CHUNKS:
            send_done(step - 1)
        if 0 <= step - 2:
            send_full(step - 2)
    for chunk in range(CHUNKS):
        pltpu.make_async_remote_copy(
            src_ref=full.at[chunk, half],
            dst_ref=full.at[chunk, 1 - half],
            send_sem=full_sem.at[0, chunk],
            recv_sem=full_sem.at[1, chunk],
            device_id=device(partner),
            device_id_type=MESH,
        ).wait_recv()
    trace = jnp.zeros((1, 1), jnp.float32)
    row_at = lax.broadcasted_iota(jnp.int32, (BLOCK, BLOCK), 0)
    col_at = lax.broadcasted_iota(jnp.int32, (BLOCK, BLOCK), 1)
    for at, (i, j) in enumerate(pairs):
        block = full[at // PAIR, at % PAIR].astype(jnp.float32)
        if i == j:
            trace += jnp.sum(jnp.where(row_at == col_at, block, 0.0), keepdims=True)
        gram[i * BLOCK : (i + 1) * BLOCK, j * BLOCK : (j + 1) * BLOCK] = block
        if i != j:
            gram[j * BLOCK : (j + 1) * BLOCK, i * BLOCK : (i + 1) * BLOCK] = block.T
    factor = 1.0 / (jnp.sqrt(trace) + EPSILON)

    def strips(step):
        @pl.loop(0, blocks)
        def _(i):
            step((slice(None), pl.ds(pl.multiple_of(i * BLOCK, BLOCK), BLOCK)))

    def scaled(cols):
        value = gram[cols] * (factor * factor)
        gram[cols] = value
        gram16[cols] = value.astype(BF16)

    def mix_first(cols):
        value = COEF_B * gram[cols] + COEF_C * dot16(gram16[...], gram16[cols])
        first[cols] = value
        first16[cols] = value.astype(BF16)

    def mix_square(cols):
        value = 2.0 * COEF_A * first[cols] + dot16(first16[...], first16[cols])
        other[cols] = value.astype(BF16)

    def next_gram(cols):
        value = COEF_A * COEF_A * gram[cols] + dot16(gram16[...], other[cols])
        gram[cols] = value
        mix[cols] = value.astype(BF16)

    def mix_second(cols):
        value = COEF_B * gram[cols] + COEF_C * dot16(mix[...], mix[cols])
        gram[cols] = value
        second16[cols] = value.astype(BF16)

    def mix_both(cols):
        value = COEF_A * (first[cols] + gram[cols]) + dot16(first16[...], second16[cols])
        top = value.astype(BF16)
        gram16[cols] = top
        mix_low[cols] = (value - top.astype(jnp.float32)).astype(BF16)

    for step in (scaled, mix_first, mix_square, next_gram, mix_second, mix_both):
        strips(step)

    stride = code.shape[1]
    parts = code.shape[0]
    locals_ = []
    group_copies = {}
    top[...] = jnp.zeros_like(top)
    for i in range(parts):
        rows = slice(i * stride, (i + 1) * stride)
        value = dot16(high[rows], gram16[...]) + dot16(low[rows], gram16[...])
        value += dot16(high[rows], mix_low[...]) + COEF_A * COEF_A * moment_ref[rows]
        value = value * (factor * scale)
        peak = jnp.maximum(jnp.max(jnp.abs(value), axis=0, keepdims=True), 1e-30)
        top[i : i + 1] = peak * (1.0 / LEVELS)
        code[i] = jnp.round(value * (LEVELS / peak)).astype(jnp.int32).astype(jnp.int16)
        place_here = code_ref.at[group, i]
        for offset in range(1, groups // PAIR):
            to = {"dp": lax.rem(group + PAIR * offset, groups)}
            group_copies[i, offset] = send(code.at[i], place_here, group_sem, (i, offset), to)
        send(code.at[i], place_here, twin_sem, (i,), {"dp": twin})
        copy = pltpu.make_async_copy(code.at[i], place_here, local_sem.at[i])
        copy.start()
        locals_.append(copy)
    for offset in range(1, groups):
        to = {"dp": lax.rem(group + offset, groups)}
        send(top, top_ref.at[group], top_sem, (offset,), to)
    copy = pltpu.make_async_copy(top, top_ref.at[group], local_sem.at[parts])
    copy.start()
    locals_.append(copy)

    def arrival(target, sems, at):
        pltpu.make_async_remote_copy(
            src_ref=target,
            dst_ref=target,
            send_sem=sems.at[(0, *at)],
            recv_sem=sems.at[(1, *at)],
            device_id={"dp": twin},
            device_id_type=MESH,
        ).wait_recv()

    for i in range(parts):
        for offset in range(1, groups // PAIR):
            source = lax.rem(group + groups - PAIR * offset, groups)
            there = code_ref.at[source, i]
            arrival(there, group_sem, (i, offset))
            send(there, there, pass_sem, (i, offset), {"dp": twin})
    for i in range(parts):
        arrival(code_ref.at[twin, i], twin_sem, (i,))
        for offset in range(1, groups // PAIR):
            source = lax.rem(twin + groups - PAIR * offset, groups)
            arrival(code_ref.at[source, i], pass_sem, (i, offset))
    for offset in range(1, groups):
        source = lax.rem(group + groups - offset, groups)
        arrival(top_ref.at[source], top_sem, (offset,))
    for copy in sends:
        copy.wait_send()
    for copy in locals_:
        copy.wait()


def iterated(moment, n, groups):
    tall, size = moment.shape
    square = (size, size)
    places = n // PAIR
    piece = BLOCK // places
    stride = math.gcd(tall, 128)
    parts = tall // stride
    tops = -(-parts // 8) * 8
    links = groups // PAIR
    vmem, dma = pltpu.VMEM, pltpu.SemaphoreType.DMA
    scratch = [vmem((tall, size), BF16)] * 2 + [
        vmem((CHUNKS, PAIR, BLOCK, BLOCK), BF16),
        vmem((CHUNKS, BLOCK, BLOCK), BF16),
        vmem((CHUNKS, BLOCK, BLOCK), BF16),
        vmem((CHUNKS, places, piece, BLOCK), BF16),
        vmem((CHUNKS, piece, BLOCK), BF16),
        vmem((CHUNKS, PAIR, BLOCK, BLOCK), BF16),
        vmem(square, jnp.float32),
        vmem(square, BF16),
        vmem(square, jnp.float32),
        vmem(square, BF16),
        vmem(square, BF16),
        vmem(square, BF16),
        vmem(square, BF16),
        vmem(square, BF16),
        vmem((parts, stride, size), jnp.int16),
        vmem((tops, size), jnp.float32),
        dma((2, CHUNKS)),
        dma((2, CHUNKS, places)),
        dma((2, CHUNKS, places)),
        dma((2, CHUNKS)),
        dma((2, parts)),
        dma((2, parts, links)),
        dma((2, parts, links)),
        dma((2, groups)),
        dma((parts + 1,)),
    ]
    code, top = pl.pallas_call(
        functools.partial(iterate_kernel, n, groups, math.sqrt(max(FF, D))),
        out_shape=(
            jax.ShapeDtypeStruct((groups, parts, stride, size), jnp.int16),
            jax.ShapeDtypeStruct((groups, tops, size), jnp.float32),
        ),
        in_specs=[pl.BlockSpec(memory_space=pltpu.VMEM)],
        out_specs=(pl.BlockSpec(memory_space=pl.ANY),) * 2,
        scratch_shapes=scratch,
        compiler_params=pltpu.CompilerParams(
            collective_id=0, has_side_effects=True, vmem_limit_bytes=56 * 2**20
        ),
    )(moment)
    return widened(code, top)


def body(hidden_token_tiles, gradient_token_tiles, momentum, filled_tile_count):
    groups = lax.axis_size("dp")
    columns_all, rows_all = exchanged(
        gradient_token_tiles, hidden_token_tiles, lax.axis_size("expert"), groups
    )
    moment = moment_of(filled_tile_count, columns_all, rows_all, momentum[0])
    update = iterated(moment, lax.axis_size("expert"), groups)
    return (moment[None], update)


def solution(mesh):
    placed = (P(None, "dp", None), P(None, "expert", "dp"), P("dp", "expert", None), P())
    return jax.shard_map(
        body,
        mesh=mesh,
        in_specs=placed,
        out_specs=(P("dp", "expert", None), P(None, "expert", None)),
        check_vma=False,
    )
```

```python
import functools
import math

import jax
import jax.numpy as jnp
from jax import lax
from jax.experimental import pallas as pl
from jax.experimental.pallas import tpu as pltpu
from jax.sharding import PartitionSpec as P

D = 7168
FF = 1024
TILE = 16
ITERS = 2


MOMENTUM_DECAY = 0.95
EPSILON = 1e-07
COEF_A = 3.4445
COEF_B = -4.775
COEF_C = 2.0315

BF16 = jnp.bfloat16
LEVELS = 32700.0
MESH = pl.DeviceIdType.MESH


BLOCK = 256
PAIR = 2
TEAM = 4
CHUNKS = 5


def dot16(left, right):
    return jnp.dot(left, right, preferred_element_type=jnp.float32)


def across(left, right):
    return lax.dot_general(left, right, (((0,), (0,)), ((), ())), preferred_element_type=jnp.float32)


def exchange_kernel(
    n, groups, tiles_ref, hidden_ref, columns_ref, rows_ref,
    twin_sem, tile_sem, piece_sem, pass_sem, local_sem,
):
    me = lax.axis_index("expert")
    group = lax.axis_index("dp")
    twin = group + 1 - 2 * lax.rem(group, PAIR)
    member = lax.rem(me, TEAM)
    team = me - member
    deep = hidden_ref.shape[1]
    piece = deep // TEAM
    hops = range(1, groups // PAIR)

    barrier = pltpu.get_barrier_semaphore()
    for offset in range(1, groups):
        to = {"dp": lax.rem(group + offset, groups)}
        pl.semaphore_signal(barrier, inc=1, device_id=to, device_id_type=MESH)
    for offset in range(1, TEAM):
        to = {"expert": team + lax.rem(member + offset, TEAM)}
        pl.semaphore_signal(barrier, inc=1, device_id=to, device_id_type=MESH)

    def slot(at):
        return columns_ref.at[:, pl.ds(pl.multiple_of(at * deep, deep), deep)]

    def strip(ref, at, which):
        return ref.at[at, pl.ds(pl.multiple_of(which * piece, piece), piece)]

    local = [
        pltpu.make_async_copy(hidden_ref.at[group], rows_ref.at[group], local_sem.at[0]),
        pltpu.make_async_copy(tiles_ref.at[group], slot(group), local_sem.at[1]),
    ]
    for copy in local:
        copy.start()
    pl.semaphore_wait(barrier, groups - 1 + TEAM - 1)

    def copy_of(source, target, sems, at, to):
        return pltpu.make_async_remote_copy(
            src_ref=source,
            dst_ref=target,
            send_sem=sems.at[(0, *at)],
            recv_sem=sems.at[(1, *at)],
            device_id=to,
            device_id_type=MESH,
        )

    sends, arrivals = [], []

    def send(*copy):
        sends.append(copy_of(*copy))
        sends[-1].start()

    def arrival(target, sems, at):
        return copy_of(target, target, sems, at, {"dp": twin})

    for hop in hops:
        for kind, base in enumerate((group, twin)):
            to = lax.rem(base + PAIR * hop, groups)
            send(
                strip(hidden_ref, to, member), strip(rows_ref, group, member),
                piece_sem, (kind, hop), {"dp": to},
            )
    for hop in hops:
        for kind, base in enumerate((group, twin)):
            to = lax.rem(base + PAIR * hop, groups)
            send(tiles_ref.at[to], slot(group), tile_sem, (kind, hop), {"dp": to})
    send(hidden_ref.at[twin], rows_ref.at[group], twin_sem, (0,), {"dp": twin})
    send(tiles_ref.at[twin], slot(group), twin_sem, (1,), {"dp": twin})
    for hop in hops:
        for kind, base in enumerate((group, twin)):
            source = lax.rem(base + groups - PAIR * hop, groups)
            mine = strip(rows_ref, source, member)
            arrival(mine, piece_sem, (kind, hop)).wait_recv()
            for offset in range(1, TEAM):
                to = {"expert": team + lax.rem(member + offset, TEAM)}
                send(mine, mine, pass_sem, (kind, hop, offset), to)
                other = lax.rem(member + TEAM - offset, TEAM)
                arrivals.append(
                    arrival(strip(rows_ref, source, other), pass_sem, (kind, hop, offset))
                )
            arrivals.append(arrival(slot(source), tile_sem, (kind, hop)))
    arrivals.append(arrival(rows_ref.at[twin], twin_sem, (0,)))
    arrivals.append(arrival(slot(twin), twin_sem, (1,)))
    for copy in arrivals:
        copy.wait_recv()
    for copy in sends:
        copy.wait_send()
    for copy in local:
        copy.wait()


def exchanged(tiles, hidden, n, groups):
    _, tall, deep = tiles.shape
    size = hidden.shape[2]
    hops = groups // PAIR
    dma = pltpu.SemaphoreType.DMA
    return pl.pallas_call(
        functools.partial(exchange_kernel, n, groups),
        out_shape=(
            jax.ShapeDtypeStruct((tall, groups * deep), BF16),
            jax.ShapeDtypeStruct((groups, deep, size), BF16),
        ),
        in_specs=[pl.BlockSpec(memory_space=pl.ANY)] * 2,
        out_specs=(pl.BlockSpec(memory_space=pl.ANY),) * 2,
        scratch_shapes=[
            dma((2, 2)),
            dma((2, 2, hops)),
            dma((2, 2, hops)),
            dma((2, 2, hops, TEAM)),
            dma((2,)),
        ],
        compiler_params=pltpu.CompilerParams(collective_id=1, has_side_effects=True),
    )(tiles, hidden)


def moment_kernel(count_ref, columns_ref, rows_ref, momentum_ref, out_ref, kept):
    group = lax.axis_index("dp")
    groups, deep, size = rows_ref.shape

    @pl.when(pl.program_id(0) == 0)
    def _():
        at = lax.broadcasted_iota(jnp.int32, (deep, size), 0)
        for source in range(groups):
            tallied = at < count_ref[source, group] * TILE
            values = jnp.where(tallied, rows_ref[source].astype(jnp.float32), 0.0)
            kept[source * deep : (source + 1) * deep] = values.astype(BF16)

    gradient = dot16(columns_ref[...], kept[...])
    out_ref[...] = MOMENTUM_DECAY * momentum_ref[...] + gradient


def moment_of(counts, columns, rows, momentum):
    tall, size = momentum.shape
    stride = tall // 2
    return pl.pallas_call(
        moment_kernel,
        grid=(tall // stride,),
        out_shape=jax.ShapeDtypeStruct(momentum.shape, jnp.float32),
        in_specs=[
            pl.BlockSpec(memory_space=pltpu.SMEM),
            pl.BlockSpec((stride, columns.shape[1]), lambda i: (i, 0)),
            pl.BlockSpec(rows.shape, lambda i: (0, 0, 0)),
            pl.BlockSpec((stride, size), lambda i: (i, 0)),
        ],
        out_specs=pl.BlockSpec((stride, size), lambda i: (i, 0)),
        scratch_shapes=[pltpu.VMEM((columns.shape[1], size), BF16)],
        compiler_params=pltpu.CompilerParams(vmem_limit_bytes=56 * 2**20),
    )(counts, columns, rows, momentum)


def widen_kernel(code_ref, top_ref, out_ref):
    for i in range(code_ref.shape[1]):
        stride = code_ref.shape[2]
        rows = slice(i * stride, (i + 1) * stride)
        out_ref[0, rows] = code_ref[0, i].astype(jnp.float32) * top_ref[0, i : i + 1]


def widened(code, top):
    groups, parts, stride, size = code.shape
    return pl.pallas_call(
        widen_kernel,
        grid=(groups,),
        out_shape=jax.ShapeDtypeStruct((groups, parts * stride, size), jnp.float32),
        in_specs=[
            pl.BlockSpec((1, parts, stride, size), lambda i: (i, 0, 0, 0)),
            pl.BlockSpec((1, top.shape[1], size), lambda i: (i, 0, 0)),
        ],
        out_specs=pl.BlockSpec((1, parts * stride, size), lambda i: (i, 0, 0)),
        compiler_params=pltpu.CompilerParams(vmem_limit_bytes=56 * 2**20),
    )(code, top)


def iterate_kernel(
    n, groups, scale, moment_ref, code_ref, top_ref, high, low, work, near, part, far, done, full,
    gram, gram16, first, first16, second16, other, mix, mix_low, code, top,
    near_sem, far_sem, done_sem, full_sem, twin_sem, group_sem, pass_sem, top_sem, local_sem,
):
    me = lax.axis_index("expert")
    group = lax.axis_index("dp")
    twin = group + 1 - 2 * lax.rem(group, PAIR)
    half, place = lax.rem(me, PAIR), lax.div(me, PAIR)
    places = n // PAIR
    piece = BLOCK // places
    partner = me + 1 - 2 * half
    size = moment_ref.shape[1]
    blocks = size // BLOCK
    pairs = [(i, j) for i in range(blocks) for j in range(i, blocks)]

    def peer(offset):
        return lax.rem(place + offset, places)

    def device(at):
        return {"expert": at}

    barrier = pltpu.get_barrier_semaphore()
    pl.semaphore_signal(barrier, inc=1, device_id=device(partner), device_id_type=MESH)
    for offset in range(1, places):
        pl.semaphore_signal(
            barrier, inc=1, device_id=device(peer(offset) * PAIR + half), device_id_type=MESH
        )

    for offset in range(1, groups):
        pl.semaphore_signal(
            barrier,
            inc=1,
            device_id={"dp": lax.rem(group + offset, groups)},
            device_id_type=MESH,
        )

    sends = []

    def send(source, target, sems, at, to):
        copy = pltpu.make_async_remote_copy(
            src_ref=source,
            dst_ref=target,
            send_sem=sems.at[(0, *at)],
            recv_sem=sems.at[(1, *at)],
            device_id=to if isinstance(to, dict) else device(to),
            device_id_type=MESH,
        )
        copy.start()
        sends.append(copy)
        return copy

    near_copies, far_copies, done_copies, full_copies = {}, {}, {}, {}

    def send_near(chunk):
        near_copies[chunk] = send(
            work.at[chunk, 1 - half], near.at[chunk], near_sem, (chunk,), partner
        )

    def send_far(chunk):
        near_copies[chunk].wait_recv()
        total = work[chunk, half].astype(jnp.float32) + near[chunk].astype(jnp.float32)
        part[chunk] = total.astype(BF16)
        for offset in range(1, places):
            to = peer(offset)
            rows = pl.ds(pl.multiple_of(to * piece, piece), piece)
            far_copies[chunk, offset] = send(
                part.at[chunk, rows],
                far.at[chunk, offset],
                far_sem,
                (chunk, offset),
                to * PAIR + half,
            )

    def send_done(chunk):
        mine = pl.ds(pl.multiple_of(place * piece, piece), piece)
        total = part[chunk, mine].astype(jnp.float32)
        for offset in range(1, places):
            far_copies[chunk, offset].wait_recv()
            total = total + far[chunk, offset].astype(jnp.float32)
        done[chunk] = total.astype(BF16)
        full[chunk, half, mine] = total.astype(BF16)
        for offset in range(1, places):
            done_copies[chunk, offset] = send(
                done.at[chunk],
                full.at[chunk, half, mine],
                done_sem,
                (chunk, offset),
                peer(offset) * PAIR + half,
            )

    def wait_done(chunk):
        for offset in range(1, places):
            source = lax.rem(place + places - offset, places)
            rows = pl.ds(pl.multiple_of(source * piece, piece), piece)
            pltpu.make_async_remote_copy(
                src_ref=done.at[chunk],
                dst_ref=full.at[chunk, half, rows],
                send_sem=done_sem.at[0, chunk, offset],
                recv_sem=done_sem.at[1, chunk, offset],
                device_id=device(partner),
                device_id_type=MESH,
            ).wait_recv()

    def send_full(chunk):
        wait_done(chunk)
        full_copies[chunk] = send(
            full.at[chunk, half], full.at[chunk, half], full_sem, (chunk,), partner
        )

    moment = moment_ref[...]
    rounded = moment.astype(BF16)
    high[...] = rounded
    low[...] = (moment - rounded.astype(jnp.float32)).astype(BF16)
    at = 0
    for i in range(blocks):
        rows = slice(i * BLOCK, (i + 1) * BLOCK)
        for start in range(i, blocks, PAIR):
            stop = min(start + PAIR, blocks)
            rest = slice(start * BLOCK, stop * BLOCK)
            strip = across(high[:, rows], high[:, rest])
            strip += across(high[:, rows], low[:, rest]) + across(low[:, rows], high[:, rest])
            for j in range(start, stop):
                block = strip[:, (j - start) * BLOCK : (j - start + 1) * BLOCK]
                work[at // PAIR, at % PAIR] = block.astype(BF16)
                at += 1
            if i == start == 0:
                pl.semaphore_wait(barrier, places + groups - 1)
            for chunk in range(len(near_copies), at // PAIR):
                send_near(chunk)
    for step in range(CHUNKS + 2):
        if step < CHUNKS:
            send_far(step)
        if 0 <= step - 1 < CHUNKS:
            send_done(step - 1)
        if 0 <= step - 2:
            send_full(step - 2)
    for chunk in range(CHUNKS):
        pltpu.make_async_remote_copy(
            src_ref=full.at[chunk, half],
            dst_ref=full.at[chunk, 1 - half],
            send_sem=full_sem.at[0, chunk],
            recv_sem=full_sem.at[1, chunk],
            device_id=device(partner),
            device_id_type=MESH,
        ).wait_recv()
    trace = jnp.zeros((1, 1), jnp.float32)
    row_at = lax.broadcasted_iota(jnp.int32, (BLOCK, BLOCK), 0)
    col_at = lax.broadcasted_iota(jnp.int32, (BLOCK, BLOCK), 1)
    for at, (i, j) in enumerate(pairs):
        if i == j:
            block = full[at // PAIR, at % PAIR].astype(jnp.float32)
            trace += jnp.sum(jnp.where(row_at == col_at, block, 0.0), keepdims=True)
    factor = 1.0 / (jnp.sqrt(trace) + EPSILON)
    for at, (i, j) in enumerate(pairs):
        block = full[at // PAIR, at % PAIR].astype(jnp.float32) * (factor * factor)
        here = (slice(i * BLOCK, (i + 1) * BLOCK), slice(j * BLOCK, (j + 1) * BLOCK))
        gram[here] = block
        gram16[here] = block.astype(BF16)
        if i != j:
            flipped = block.T
            gram[here[::-1]] = flipped
            gram16[here[::-1]] = flipped.astype(BF16)

    def strips(step):
        @pl.loop(0, blocks)
        def _(i):
            step((slice(None), pl.ds(pl.multiple_of(i * BLOCK, BLOCK), BLOCK)))

    def mix_first(cols):
        value = COEF_B * gram[cols] + COEF_C * dot16(gram16[...], gram16[cols])
        first[cols] = value
        first16[cols] = value.astype(BF16)

    def mix_square(cols):
        value = 2.0 * COEF_A * first[cols] + dot16(first16[...], first16[cols])
        other[cols] = value.astype(BF16)

    def next_gram(cols):
        value = COEF_A * COEF_A * gram[cols] + dot16(gram16[...], other[cols])
        gram[cols] = value
        mix[cols] = value.astype(BF16)

    def mix_second(cols):
        value = COEF_B * gram[cols] + COEF_C * dot16(mix[...], mix[cols])
        gram[cols] = value
        second16[cols] = value.astype(BF16)

    def mix_both(cols):
        value = COEF_A * (first[cols] + gram[cols]) + dot16(first16[...], second16[cols])
        top = value.astype(BF16)
        gram16[cols] = top
        mix_low[cols] = (value - top.astype(jnp.float32)).astype(BF16)

    for step in (mix_first, mix_square, next_gram, mix_second, mix_both):
        strips(step)

    stride = code.shape[1]
    parts = code.shape[0]
    locals_ = []
    group_copies = {}
    top[...] = jnp.zeros_like(top)
    for i in range(parts):
        rows = slice(i * stride, (i + 1) * stride)
        value = dot16(high[rows], gram16[...]) + dot16(low[rows], gram16[...])
        value += dot16(high[rows], mix_low[...]) + COEF_A * COEF_A * moment_ref[rows]
        value = value * (factor * scale)
        peak = jnp.maximum(jnp.max(jnp.abs(value), axis=0, keepdims=True), 1e-30)
        top[i : i + 1] = peak * (1.0 / LEVELS)
        code[i] = jnp.round(value * (LEVELS / peak)).astype(jnp.int32).astype(jnp.int16)
        place_here = code_ref.at[group, i]
        for offset in range(1, groups // PAIR):
            to = {"dp": lax.rem(group + PAIR * offset, groups)}
            group_copies[i, offset] = send(code.at[i], place_here, group_sem, (i, offset), to)
        send(code.at[i], place_here, twin_sem, (i,), {"dp": twin})
        copy = pltpu.make_async_copy(code.at[i], place_here, local_sem.at[i])
        copy.start()
        locals_.append(copy)
    for offset in range(1, groups):
        to = {"dp": lax.rem(group + offset, groups)}
        send(top, top_ref.at[group], top_sem, (offset,), to)
    copy = pltpu.make_async_copy(top, top_ref.at[group], local_sem.at[parts])
    copy.start()
    locals_.append(copy)

    def arrival(target, sems, at):
        pltpu.make_async_remote_copy(
            src_ref=target,
            dst_ref=target,
            send_sem=sems.at[(0, *at)],
            recv_sem=sems.at[(1, *at)],
            device_id={"dp": twin},
            device_id_type=MESH,
        ).wait_recv()

    for i in range(parts):
        for offset in range(1, groups // PAIR):
            source = lax.rem(group + groups - PAIR * offset, groups)
            there = code_ref.at[source, i]
            arrival(there, group_sem, (i, offset))
            send(there, there, pass_sem, (i, offset), {"dp": twin})
    for i in range(parts):
        arrival(code_ref.at[twin, i], twin_sem, (i,))
        for offset in range(1, groups // PAIR):
            source = lax.rem(twin + groups - PAIR * offset, groups)
            arrival(code_ref.at[source, i], pass_sem, (i, offset))
    for offset in range(1, groups):
        source = lax.rem(group + groups - offset, groups)
        arrival(top_ref.at[source], top_sem, (offset,))
    for copy in sends:
        copy.wait_send()
    for copy in locals_:
        copy.wait()


def iterated(moment, n, groups):
    tall, size = moment.shape
    square = (size, size)
    places = n // PAIR
    piece = BLOCK // places
    stride = math.gcd(tall, 128)
    parts = tall // stride
    tops = -(-parts // 8) * 8
    links = groups // PAIR
    vmem, dma = pltpu.VMEM, pltpu.SemaphoreType.DMA
    scratch = [vmem((tall, size), BF16)] * 2 + [
        vmem((CHUNKS, PAIR, BLOCK, BLOCK), BF16),
        vmem((CHUNKS, BLOCK, BLOCK), BF16),
        vmem((CHUNKS, BLOCK, BLOCK), BF16),
        vmem((CHUNKS, places, piece, BLOCK), BF16),
        vmem((CHUNKS, piece, BLOCK), BF16),
        vmem((CHUNKS, PAIR, BLOCK, BLOCK), BF16),
        vmem(square, jnp.float32),
        vmem(square, BF16),
        vmem(square, jnp.float32),
        vmem(square, BF16),
        vmem(square, BF16),
        vmem(square, BF16),
        vmem(square, BF16),
        vmem(square, BF16),
        vmem((parts, stride, size), jnp.int16),
        vmem((tops, size), jnp.float32),
        dma((2, CHUNKS)),
        dma((2, CHUNKS, places)),
        dma((2, CHUNKS, places)),
        dma((2, CHUNKS)),
        dma((2, parts)),
        dma((2, parts, links)),
        dma((2, parts, links)),
        dma((2, groups)),
        dma((parts + 1,)),
    ]
    code, top = pl.pallas_call(
        functools.partial(iterate_kernel, n, groups, math.sqrt(max(FF, D))),
        out_shape=(
            jax.ShapeDtypeStruct((groups, parts, stride, size), jnp.int16),
            jax.ShapeDtypeStruct((groups, tops, size), jnp.float32),
        ),
        in_specs=[pl.BlockSpec(memory_space=pltpu.VMEM)],
        out_specs=(pl.BlockSpec(memory_space=pl.ANY),) * 2,
        scratch_shapes=scratch,
        compiler_params=pltpu.CompilerParams(
            collective_id=0, has_side_effects=True, vmem_limit_bytes=56 * 2**20
        ),
    )(moment)
    return widened(code, top)


def body(hidden_token_tiles, gradient_token_tiles, momentum, filled_tile_count):
    groups = lax.axis_size("dp")
    columns_all, rows_all = exchanged(
        gradient_token_tiles, hidden_token_tiles, lax.axis_size("expert"), groups
    )
    moment = moment_of(filled_tile_count, columns_all, rows_all, momentum[0])
    update = iterated(moment, lax.axis_size("expert"), groups)
    return (moment[None], update)


def solution(mesh):
    placed = (P(None, "dp", None), P(None, "expert", "dp"), P("dp", "expert", None), P())
    return jax.shard_map(
        body,
        mesh=mesh,
        in_specs=placed,
        out_specs=(P("dp", "expert", None), P(None, "expert", None)),
        check_vma=False,
    )
```
